32 devices in a mesh: groups: 2 (over y), tm: 4 (over z), heads: 4 (over x, core).
Axes of the slice: x: 2, y: 2, z: 4, core: 2. Of those that a mesh axis runs over, the one named last changes fastest.
Arguments:
- wave_feats: bfloat16 [5120, 512], P(('groups', 'tm')), parts along dimension 0, may hold values from -6 to 6
- conv_weight: bfloat16 [2, 512, 512], P(None, None, 'heads'), may hold values from -0.1875 to 0.1875
- proj_weight: bfloat16 [512, 1280], P('heads'), may hold values from -0.25 to 0.25
- ln_gain: float32 [1280], replicated, may hold values from 0.1 to 1.9
- qkv_weight: bfloat16 [1280, 3, 1280], P(None, None, 'heads'), may hold values from -1 to 1
- out_weight: bfloat16 [1280, 1280], P(None, 'heads'), may hold values from -0.15625 to 0.15625
- depth_weight: float32 [31, 1280], P(None, 'heads'), may hold values from -1 to 1
- depth_scale: float32 [1280], P('heads'), may hold values from 0.5 to 2
- depth_shift: float32 [1280], P('heads'), may hold values from -3 to 3
- seg_ids: int32 [2560], P('groups'), parts along dimension 0, may hold values from 0 to 7, never falling along the last dimension, each value on 1 to 320 neighbouring positions
- phrase_ids: int32 [8, 512], P('groups'), parts along dimension 0, may hold values from 0 to 8191, as said below
- counts: int32 [8], P('groups'), parts along dimension 0, may hold values from 1 to 512, 1024 in all
- phrase_store: bfloat16 [8192, 2, 1280], P('tm', None, 'heads'), may hold values from -9 to 9
Outputs:
- scored: bfloat16 [2560, 1280], P(('groups', 'tm'), 'heads'), parts along dimension 0
The draws below stay inside these ranges and needn't reach their ends.
There are 2 independent parts, one for each index of `groups`. The reference program is written for one: setup_inputs(seed, part) draws one part's arguments, and reference() takes and returns one part's arrays. A program takes and returns all parts, laid end to end along the dimension named above; an argument that names none is the same for every part. Nothing has to cross between parts.
Inputs may be any that keep to these rules, and one draw needn't show every extreme that they name: `phrase_ids`: each segment's list names phrases of exactly 2 owners, exactly 256 slots for each of them, the owner of phrase p being p // 2048; ids may repeat.
All inputs are finite; a program needn't handle non-finite values.
Results may differ from the reference program's by a relative error of at most 0.0085.
The reference program's roundings to bfloat16 on the way count: a program that leaves them out, or rounds other values in their place, can miss the bound.
Values may be sent and summed in bfloat16 or wider, within the bound.
A program may use at most 64 MiB of HBM per device.

```python
import math
import jax
import jax.numpy as jnp
import numpy as np
from jax import lax

CH = 512
D = 1280
HEADS = 20
HEAD_DIM = 64
KERNEL = 31
SEG = 320
LIST = 512
PHRASES = 8192
SEGMENTS = 4
FRAMES = 1280
HALF = 15
CAP = 256
PH_DEV = 2048


def draw_phrase_ids(key, part):
    row_keys = jax.random.split(jax.random.fold_in(key, 11), SEGMENTS)

    def one_row(row_key):
        owner_key, local_key, order_key = jax.random.split(row_key, 3)
        chosen = jax.random.permutation(owner_key, SEGMENTS)[:LIST // CAP]
        slot_owner = jnp.repeat(chosen, CAP)
        local_rows = jax.random.randint(local_key, (LIST,), 0, PH_DEV)
        order = jax.random.permutation(order_key, LIST)
        return (slot_owner * PH_DEV + local_rows)[order]
    return jax.vmap(one_row)(row_keys).astype(jnp.int32)


def column_signs(key):
    picked = jax.random.bernoulli(jax.random.fold_in(key, 501), 0.5, (D,))
    return jnp.where(picked, 1.0, -1.0).astype(jnp.float32)


def draw_qkv_weight(key, part):
    base_key = jax.random.fold_in(key, 21)
    direction_key = jax.random.fold_in(key, 22)
    root_three = math.sqrt(3.0)
    base = jnp.clip(jax.random.normal(base_key, (D, 3, D), jnp.float32), -4.0, 4.0)
    base = base * (1.0 / math.sqrt(D))
    direction = jax.random.uniform(direction_key, (HEADS, D), jnp.float32, -root_three, root_three) * (1.0 / math.sqrt(D))
    per_column = jnp.repeat(direction, HEAD_DIM, axis=0)
    strength = 7.5 / math.sqrt(HEAD_DIM)
    planted = strength * jnp.transpose(per_column) * column_signs(key)[None, :]
    return base.at[:, 0, :].add(planted).astype(jnp.bfloat16)


def draw_phrase_store(key, part):
    base_key = jax.random.fold_in(key, 31)
    pick_key = jax.random.fold_in(key, 32)
    level_key = jax.random.fold_in(key, 33)
    base = jnp.clip(1.5 * jax.random.normal(base_key, (PHRASES, 2, D), jnp.float32), -9.0, 9.0)
    picked = jax.random.bernoulli(pick_key, 1.0 / 16.0, (PHRASES,))
    level = 0.95 + 0.05 * jax.random.uniform(level_key, (PHRASES,), jnp.float32)
    aligned = 9.0 * level[:, None] * column_signs(key)[None, :]
    key_half = jnp.where(picked[:, None], aligned, base[:, 0])
    return jnp.stack([key_half, base[:, 1]], axis=1).astype(jnp.bfloat16)


def block_scale(key, dims, cuts, least, top_value):
    def one(dim, shards_of):
        steps = jax.random.uniform(jax.random.fold_in(jax.random.fold_in(key, 6), dim), (shards_of,), jnp.float32, least / len(cuts), top_value / len(cuts))
        return jnp.repeat(jnp.exp(steps), dims[dim] // shards_of).reshape((-1,) + (1,) * (len(dims) - dim - 1))

    factor_of = one(*cuts[0])
    for cut in cuts[1:]:
        factor_of = factor_of * one(*cut)
    return factor_of


def split_up(count, total, limit, lean):
    weights = [(1 << 20) // math.isqrt(grade ** lean) + 1 for grade in range(2, count + 1)]
    rest, holding = total - limit - (count - 1), [1] * (count - 1)
    while rest > 0:
        candidates = [i for i in range(count - 1) if holding[i] < limit]
        whole, left = sum([weights[i] for i in candidates]), rest
        for i in candidates:
            addition = min(limit - holding[i], max(1, left * weights[i] // whole), rest)
            holding[i] = holding[i] + addition
            rest = rest - addition
    return np.array([limit] + holding)


def uneven_parts(rng, number_of, total, bound, lean):
    if number_of == 2:
        one = jax.random.randint(rng, (), max(1, total - bound), min(bound, total - 1) + 1)
        return jnp.stack([one, total - one])
    tallies = jnp.asarray(split_up(number_of, total, bound, lean), jnp.int32)
    couples = (number_of - 1) // 2
    donor, taker = tallies[1:1 + 2 * couples:2], tallies[2:2 + 2 * couples:2]
    margin = jnp.minimum(donor - 1, bound - taker)
    shifted = jax.random.randint(jax.random.fold_in(rng, 1), (couples,), 0, 1 << 20) % (margin + 1)
    tallies = tallies.at[1:1 + 2 * couples:2].set(donor - shifted).at[2:2 + 2 * couples:2].set(taker + shifted)
    return tallies[jax.random.permutation(jax.random.fold_in(rng, 2), number_of)]


def normal_values(stream_key, extent, deviation, reach, shards=(), kind=jnp.bfloat16):
    result = jax.random.normal(stream_key, extent, jnp.float32) * deviation
    if len(shards) > 0:
        result = block_scale(stream_key, extent, shards, -0.22, 0.18) * result
    return jnp.clip(result, min=-reach, max=reach).astype(kind)


def setup_inputs(seed: int = 0, part: int = 0) -> dict:
    key_list = jax.random.split(jax.random.key(seed), 14)
    part_splits = jax.random.split(jax.random.fold_in(key_list[13], part), 14)
    wave_feats = normal_values(part_splits[0], (2 * FRAMES, CH), 1.0, 6.0, ((0, 4),))
    conv_weight = normal_values(key_list[1], (2, CH, CH), (2 * CH) ** -0.5, 0.1875, ((2, 4),))
    proj_weight = normal_values(key_list[2], (CH, D), CH ** -0.5, 0.25, ((0, 4),))
    ln_gain = jnp.clip(1.0 + 0.18 * jax.random.normal(key_list[3], (D,), jnp.float32), 0.1, 1.9)
    qkv_weight = draw_qkv_weight(jax.random.fold_in(key_list[13], 71), part)
    out_weight = normal_values(key_list[5], (D, D), D ** -0.5, 0.15625, ((1, 4),))
    depth_weight = normal_values(key_list[6], (KERNEL, D), KERNEL ** -0.5, 1.0, ((1, 4),), jnp.float32)
    depth_scale = jnp.clip(jnp.exp(math.log(2.0) - 1.3862944 * jax.random.uniform(key_list[7], (D,), jnp.float32) ** block_scale(key_list[7], (D,), ((0, 4),), -0.2, 0.2)), 0.5, 2.0)
    depth_shift = normal_values(key_list[8], (D,), 0.5, 3.0, ((0, 4),), jnp.float32)
    seg_ids = jnp.searchsorted(jnp.cumsum(uneven_parts(part_splits[9], 2 * SEGMENTS, FRAMES, SEG, 2)), jnp.arange(FRAMES), side="right").astype(jnp.int32)
    phrase_ids = draw_phrase_ids(jax.random.fold_in(jax.random.fold_in(key_list[13], part), 71), part)
    counts = uneven_parts(part_splits[11], SEGMENTS, SEGMENTS * LIST // 2, LIST, 2).astype(jnp.int32)
    phrase_store = draw_phrase_store(jax.random.fold_in(key_list[13], 71), part)
    return {"wave_feats": wave_feats, "conv_weight": conv_weight, "proj_weight": proj_weight, "ln_gain": ln_gain, "qkv_weight": qkv_weight, "out_weight": out_weight, "depth_weight": depth_weight, "depth_scale": depth_scale, "depth_shift": depth_shift, "seg_ids": seg_ids, "phrase_ids": phrase_ids, "counts": counts, "phrase_store": phrase_store}


def layer_norm(values, gain):
    centre = lax.optimization_barrier(jnp.mean(values, axis=-1, keepdims=True))
    centred = values - centre
    variance = lax.optimization_barrier(jnp.mean(centred * centred, axis=-1, keepdims=True))
    return centred * lax.rsqrt(variance + 1e-05) * gain

def attend(queries, keys_all, values_all, allowed):
    query_heads = queries.astype(jnp.float32).reshape(queries.shape[0], -1, HEAD_DIM)
    key_heads = keys_all.astype(jnp.float32).reshape(keys_all.shape[0], -1, HEAD_DIM)
    value_heads = values_all.astype(jnp.float32).reshape(values_all.shape[0], -1, HEAD_DIM)
    scores = jnp.einsum('qhd,khd->hqk', query_heads, key_heads) / math.sqrt(HEAD_DIM)
    scores = jnp.where(allowed[None], scores, -1e+30)
    highest = lax.optimization_barrier(jnp.max(scores, axis=-1, keepdims=True))
    raised = jnp.where(allowed[None], jnp.exp(scores - highest), 0.0)
    weights = (raised / lax.optimization_barrier(jnp.sum(raised, axis=-1, keepdims=True))).astype(jnp.bfloat16)
    output = jnp.einsum('hqk,khd->qhd', weights.astype(jnp.float32), value_heads)
    return output.reshape(queries.shape[0], -1).astype(jnp.bfloat16)

def reference(wave_feats, conv_weight, proj_weight, ln_gain, qkv_weight, out_weight, depth_weight, depth_scale, depth_shift, seg_ids, phrase_ids, counts, phrase_store):
    frame_pairs = wave_feats.reshape(FRAMES, 2 * CH)
    conv_out = jax.nn.gelu(jnp.dot(frame_pairs, conv_weight.reshape(2 * CH, CH), preferred_element_type=jnp.float32), approximate=False).astype(jnp.bfloat16)
    hidden = jnp.dot(conv_out, proj_weight, preferred_element_type=jnp.float32).astype(jnp.bfloat16)
    normed = layer_norm(hidden.astype(jnp.float32), ln_gain).astype(jnp.bfloat16)
    proj_qkv = jnp.dot(normed, qkv_weight.reshape(D, 3 * D), preferred_element_type=jnp.float32).astype(jnp.bfloat16).reshape(FRAMES, 3, D)
    queries_all = proj_qkv[:, 0]
    padded_kv = jnp.pad(proj_qkv[:, 1:3], ((SEG, SEG), (0, 0), (0, 0)))
    padded_ids = jnp.pad(seg_ids, (SEG, SEG), constant_values=-1)
    fetched = phrase_store[phrase_ids]

    def one_segment(segment):
        first_frame = (segment * SEG).astype(jnp.int32)
        queries = lax.dynamic_slice_in_dim(queries_all, first_frame, SEG, 0)
        window_kv = lax.dynamic_slice_in_dim(padded_kv, first_frame, 3 * SEG, 0)
        window_ids = lax.dynamic_slice_in_dim(padded_ids, first_frame, 3 * SEG, 0)
        own_ids = lax.dynamic_slice_in_dim(seg_ids, first_frame, SEG, 0)
        phrase_kv = lax.dynamic_index_in_dim(fetched, segment, 0, keepdims=False)
        live_slots = jnp.arange(LIST, dtype=jnp.int32) < counts[segment]
        frame_mask = own_ids[:, None] == window_ids[None, :]
        allowed = jnp.concatenate([frame_mask, jnp.broadcast_to(live_slots[None, :], (SEG, LIST))], axis=1)
        keys_all = jnp.concatenate([window_kv[:, 0], phrase_kv[:, 0]], axis=0)
        values_all = jnp.concatenate([window_kv[:, 1], phrase_kv[:, 1]], axis=0)
        return attend(queries, keys_all, values_all, allowed)
    attended = lax.map(one_segment, jnp.arange(SEGMENTS, dtype=jnp.int32)).reshape(FRAMES, D)
    mixed = (hidden.astype(jnp.float32) + jnp.dot(attended, out_weight, preferred_element_type=jnp.float32)).astype(jnp.bfloat16)
    widened = jnp.pad(mixed.astype(jnp.float32), ((HALF, HALF), (0, 0)))
    depth_sum = jnp.zeros((FRAMES, D), jnp.float32)
    for tap_index in range(KERNEL):
        depth_sum = depth_sum + widened[tap_index:tap_index + FRAMES] * depth_weight[tap_index]
    return (mixed.astype(jnp.float32) + jax.nn.silu(depth_sum * depth_scale + depth_shift)).astype(jnp.bfloat16)
```

```python
import functools
import math

import jax
import jax.numpy as jnp
from jax import lax
from jax.experimental import pallas as pl
from jax.experimental.pallas import tpu as pltpu
from jax.sharding import PartitionSpec as P

HEAD_DIM = 64
EDGE = 16
BLOCKS = 2
NEG = -1e30
F32 = jnp.float32
BF16 = jnp.bfloat16


def dot_nt(a, b):
    return lax.dot_general(a, b, (((1,), (1,)), ((), ())), preferred_element_type=F32)


def dot_nn(a, b):
    return lax.dot_general(a, b, (((1,), (0,)), ((), ())), preferred_element_type=F32)


def kernel(
    segments,
    cap,
    owners_ref,
    wave_ref,
    conv_ref,
    proj_ref,
    gain_ref,
    wqkv_hbm,
    wout_hbm,
    taps_ref,
    scale_ref,
    shift_ref,
    own_ids_ref,
    win_ids_ref,
    slot_bias_ref,
    requests_ref,
    store_hbm,
    out_ref,
    store,
    wqkv,
    wout,
    picked,
    landed,
    proj_all,
    conv_all,
    conv_pre,
    hidden,
    normed,
    queries,
    kv,
    phrases,
    bias,
    attended,
    mixed,
    wide,
    load_sem,
    proj_send,
    proj_recv,
    conv_send,
    conv_recv,
    pick_send,
    pick_recv,
    kv_send,
    kv_recv,
    att_send,
    att_recv,
    mix_send,
    mix_recv,
):
    rows, cols = out_ref.shape
    slots = phrases.shape[1]
    me = lax.axis_index("heads")
    seg = lax.axis_index("tm")
    near = me + 1 - 2 * (me % 2)
    far = (me + 2) % 4

    def remote(src, dst, send, recv, **where):
        return pltpu.make_async_remote_copy(
            src_ref=src,
            dst_ref=dst,
            send_sem=send,
            recv_sem=recv,
            device_id=where,
            device_id_type=pl.DeviceIdType.MESH,
        )

    loads = [
        pltpu.make_async_copy(store_hbm, store, load_sem.at[0]),
        pltpu.make_async_copy(wqkv_hbm, wqkv, load_sem.at[1]),
        pltpu.make_async_copy(wout_hbm, wout, load_sem.at[2]),
    ]
    for load in loads:
        load.start()

    barrier = pltpu.get_barrier_semaphore()
    for peer in (near, far):
        pl.semaphore_signal(
            barrier, inc=1, device_id={"heads": peer}, device_id_type=pl.DeviceIdType.MESH
        )
    for step in range(1, segments):
        pl.semaphore_signal(
            barrier,
            inc=1,
            device_id={"tm": (seg + step) % segments},
            device_id_type=pl.DeviceIdType.MESH,
        )
    pl.semaphore_wait(barrier, segments + 1)

    proj_copies = [
        remote(proj_ref, proj_all.at[me], proj_send.at[0], proj_recv.at[0], heads=near),
        remote(proj_ref, proj_all.at[me], proj_send.at[1], proj_recv.at[1], heads=far),
        remote(proj_all.at[far], proj_all.at[far], proj_send.at[2], proj_recv.at[2], heads=near),
    ]
    proj_copies[1].start()
    proj_copies[0].start()
    proj_all[me] = proj_ref[...]

    group = conv_ref.shape[2]
    both = jnp.concatenate([conv_ref[0], conv_ref[1]], axis=1)
    taps_out = dot_nn(wave_ref[...], both)
    conv_pre[0] = taps_out[:, :group]
    conv_pre[1] = taps_out[:, group:]
    total = conv_pre[0, pl.ds(0, rows, stride=2), :] + conv_pre[1, pl.ds(1, rows, stride=2), :]
    gelu = 0.5 * total * (1.0 + lax.erf(total * math.sqrt(0.5)))
    conv_all[me] = gelu.astype(BF16)
    conv_copies = [
        remote(conv_all.at[me], conv_all.at[me], conv_send.at[0], conv_recv.at[0], heads=near),
        remote(conv_all.at[me], conv_all.at[me], conv_send.at[1], conv_recv.at[1], heads=far),
        remote(conv_all.at[far], conv_all.at[far], conv_send.at[2], conv_recv.at[2], heads=near),
    ]
    conv_copies[1].start()
    conv_copies[0].start()

    loads[0].wait()
    chunk = max(cap, 256)
    per_chunk = chunk // cap
    store_rows = store.shape[1]
    for at in range(segments * cap // chunk):
        wanted = requests_ref[0:1, at * chunk : (at + 1) * chunk]
        place = lax.broadcasted_iota(jnp.int32, (store_rows, chunk), 0)
        hot = jnp.where(place == wanted, 1.0, 0.0).astype(BF16)
        found = dot_nn(store[...], hot).astype(BF16)
        for part in range(per_chunk):
            picked[at * per_chunk + part] = found[:, part * cap : (part + 1) * cap]
    pick_copies = []
    for step in range(1, segments):
        target = (seg + step) % segments
        copy = remote(
            picked.at[target], landed.at[seg], pick_send.at[step], pick_recv.at[step], tm=target
        )
        copy.start()
        pick_copies.append(copy)
    landed[seg] = picked[seg]

    same = own_ids_ref[...] == win_ids_ref[...]
    bias[:, : 3 * rows] = jnp.where(same, 0.0, NEG)
    bias[:, 3 * rows :] = jnp.broadcast_to(slot_bias_ref[...], (rows, slots))

    conv_copies[1].wait_recv()
    conv_copies[2].start()
    proj_copies[1].wait_recv()
    proj_copies[2].start()
    conv_copies[0].wait_recv()
    proj_copies[0].wait_recv()
    conv_copies[2].wait_recv()
    proj_copies[2].wait_recv()
    conv_full = jnp.concatenate([conv_all[r] for r in range(4)], axis=1)
    weight_full = proj_all[...].reshape(4 * group, proj_ref.shape[1])
    hidden[...] = dot_nn(conv_full, weight_full).astype(BF16)

    def norm(block, carry):
        at = pl.ds(pl.multiple_of(block * 64, 64), 64)
        values = hidden[at, :].astype(F32)
        centred = values - jnp.mean(values, axis=-1, keepdims=True)
        variance = jnp.mean(centred * centred, axis=-1, keepdims=True)
        normed[at, :] = (centred * lax.rsqrt(variance + 1e-05) * gain_ref[...]).astype(BF16)
        return carry

    lax.fori_loop(0, rows // 64, norm, 0)

    loads[1].wait()
    kv[rows : 2 * rows, :cols] = dot_nt(normed[...], wqkv[1]).astype(BF16)
    kv[rows : 2 * rows, cols:] = dot_nt(normed[...], wqkv[2]).astype(BF16)
    own_kv = kv.at[pl.ds(rows, rows)]
    kv_down = remote(
        own_kv, kv.at[pl.ds(0, rows)], kv_send.at[0], kv_recv.at[0], tm=(seg + 1) % segments
    )
    kv_up = remote(
        own_kv,
        kv.at[pl.ds(2 * rows, rows)],
        kv_send.at[1],
        kv_recv.at[1],
        tm=(seg + segments - 1) % segments,
    )
    first = seg == 0
    last = seg == segments - 1
    inner_low = seg > 0
    inner_high = seg < segments - 1

    @pl.when(inner_high)
    def _():
        kv_down.start()

    @pl.when(inner_low)
    def _():
        kv_up.start()

    @pl.when(first)
    def _():
        kv[:rows, :] = jnp.zeros((rows, 2 * cols), BF16)

    @pl.when(last)
    def _():
        kv[2 * rows :, :] = jnp.zeros((rows, 2 * cols), BF16)

    queries[...] = (dot_nt(normed[...], wqkv[0]).astype(BF16) * HEAD_DIM**-0.5).astype(BF16)

    for copy in pick_copies:
        copy.wait_recv()
    for use in range(slots // cap):
        phrases[:, use * cap : (use + 1) * cap] = landed[owners_ref[use]]

    @pl.when(inner_low)
    def _():
        kv_down.wait_recv()

    @pl.when(inner_high)
    def _():
        kv_up.wait_recv()

    step_rows = rows // BLOCKS

    def att_copies(block):
        at = pl.ds(pl.multiple_of(block * step_rows, 32), step_rows)
        mine, others = attended.at[me, at], attended.at[far, at]
        return [
            remote(mine, mine, att_send.at[block, 0], att_recv.at[block, 0], heads=near),
            remote(mine, mine, att_send.at[block, 1], att_recv.at[block, 1], heads=far),
            remote(others, others, att_send.at[block, 2], att_recv.at[block, 2], heads=near),
        ]

    def forward(block):
        copies = att_copies(block)
        copies[1].wait_recv()
        copies[2].start()

    def attend(block, carry):
        at = pl.ds(pl.multiple_of(block * step_rows, 32), step_rows)
        for head in range(cols // HEAD_DIM):
            low, high = head * HEAD_DIM, (head + 1) * HEAD_DIM
            query = queries[at, low:high]
            frame_scores = dot_nt(query, kv[:, low:high]) + bias[at, : 3 * rows]
            slot_scores = dot_nn(query, phrases[low:high, :]) + bias[at, 3 * rows :]
            highest = jnp.maximum(
                jnp.max(frame_scores, axis=-1, keepdims=True),
                jnp.max(slot_scores, axis=-1, keepdims=True),
            )
            frame_raised = jnp.exp(frame_scores - highest)
            slot_raised = jnp.exp(slot_scores - highest)
            whole = jnp.sum(frame_raised, axis=-1, keepdims=True) + jnp.sum(
                slot_raised, axis=-1, keepdims=True
            )
            summed = dot_nn(frame_raised.astype(BF16), kv[:, cols + low : cols + high]) + dot_nt(
                slot_raised.astype(BF16), phrases[cols + low : cols + high, :]
            )
            attended[me, at, low:high] = (summed / whole).astype(BF16)
        copies = att_copies(block)
        copies[1].start()
        copies[0].start()

        @pl.when(block > 0)
        def _():
            forward(block - 1)

        return carry

    lax.fori_loop(0, BLOCKS, attend, 0)
    forward(BLOCKS - 1)

    loads[2].wait()
    own = hidden[:, :cols]
    for r in range(1, 4):
        own = jnp.where(me == r, hidden[:, r * cols : (r + 1) * cols], own)
    for block in range(BLOCKS):
        copies = att_copies(block)
        copies[0].wait_recv()
        copies[2].wait_recv()
    attended_full = jnp.concatenate([attended[r] for r in range(4)], axis=1)
    product = dot_nt(attended_full, wout[...])
    mixed[EDGE : EDGE + rows, :] = (own.astype(F32) + product).astype(BF16)

    mix_down = remote(
        mixed.at[pl.ds(rows, EDGE)],
        mixed.at[pl.ds(0, EDGE)],
        mix_send.at[0],
        mix_recv.at[0],
        tm=(seg + 1) % segments,
    )
    mix_up = remote(
        mixed.at[pl.ds(EDGE, EDGE)],
        mixed.at[pl.ds(EDGE + rows, EDGE)],
        mix_send.at[1],
        mix_recv.at[1],
        tm=(seg + segments - 1) % segments,
    )

    @pl.when(inner_high)
    def _():
        mix_down.start()

    @pl.when(inner_low)
    def _():
        mix_up.start()

    @pl.when(first)
    def _():
        mixed[:EDGE, :] = jnp.zeros((EDGE, cols), BF16)

    @pl.when(last)
    def _():
        mixed[EDGE + rows :, :] = jnp.zeros((EDGE, cols), BF16)

    wide[EDGE : EDGE + rows, :] = mixed[EDGE : EDGE + rows, :].astype(F32)

    for copy in proj_copies + conv_copies + pick_copies:
        copy.wait_send()
    for block in range(BLOCKS):
        for copy in att_copies(block):
            copy.wait_send()

    @pl.when(inner_high)
    def _():
        kv_down.wait_send()
        mix_down.wait_send()
        mix_up.wait_recv()

    @pl.when(inner_low)
    def _():
        kv_up.wait_send()
        mix_up.wait_send()
        mix_down.wait_recv()

    wide[:EDGE, :] = mixed[:EDGE, :].astype(F32)
    wide[EDGE + rows :, :] = mixed[EDGE + rows :, :].astype(F32)

    kernel_taps = taps_ref.shape[0]
    lead = EDGE - kernel_taps // 2
    for top in range(0, rows, 64):
        depth = jnp.zeros((64, cols), F32)
        for tap in range(kernel_taps):
            start = top + tap + lead
            depth = depth + wide[start : start + 64, :] * taps_ref[tap : tap + 1, :]
        gated = depth * scale_ref[...] + shift_ref[...]
        value = wide[EDGE + top : EDGE + top + 64, :] + gated / (1.0 + jnp.exp(-gated))
        out_ref[top : top + 64, :] = value.astype(BF16)


def body(
    wave_feats,
    conv_weight,
    proj_weight,
    ln_gain,
    qkv_weight,
    out_weight,
    depth_weight,
    depth_scale,
    depth_shift,
    seg_ids,
    phrase_ids,
    counts,
    phrase_store,
):
    rows = wave_feats.shape[0] // 2
    cols = qkv_weight.shape[2]
    width = qkv_weight.shape[0]
    group = proj_weight.shape[0]
    segment = lax.axis_index("tm")
    segments = lax.axis_size("tm")
    slots = phrase_ids.shape[1]
    cap = 2 * slots // segments
    store_rows = phrase_store.shape[0]

    padded_ids = jnp.pad(seg_ids, (rows, rows), constant_values=-1)
    win_ids = lax.dynamic_slice_in_dim(padded_ids, segment * rows, 3 * rows, 0)
    own_ids = lax.dynamic_slice_in_dim(seg_ids, segment * rows, rows, 0)

    owners = lax.div(phrase_ids, store_rows)
    local = phrase_ids - owners * store_rows
    order = jnp.arange(slots, dtype=jnp.int32)
    earlier = order[:, None] < order[None, :]
    held = owners == segment
    rank = jnp.sum(
        jnp.logical_and(held[:, :, None], earlier[None]).astype(jnp.int32), axis=1
    )
    rank = jnp.where(held, rank, cap)
    ranks = jnp.arange(cap, dtype=jnp.int32)
    requests = jnp.sum(
        jnp.where(rank[:, :, None] == ranks[None, None, :], local[:, :, None], 0), axis=1
    ).reshape(1, segments * cap)

    my_owner = lax.dynamic_index_in_dim(owners, segment, 0, keepdims=False)
    every = jnp.arange(segments, dtype=jnp.int32)
    listed = my_owner[None, :] == every[:, None]
    live = jnp.sum(
        jnp.logical_and(listed, order[None, :] < counts[segment]).astype(jnp.int32), axis=1
    )
    present = jnp.any(listed, axis=1)
    before = jnp.sum(
        jnp.logical_and(present[None, :], every[None, :] < every[:, None]).astype(jnp.int32), axis=1
    )
    uses = jnp.arange(slots // cap, dtype=jnp.int32)
    chosen = jnp.logical_and(present[None, :], before[None, :] == uses[:, None]).astype(jnp.int32)
    owner_list = jnp.sum(chosen * every[None, :], axis=1)
    live_list = jnp.sum(chosen * live[None, :], axis=1)
    slot_bias = jnp.where(ranks[None, :] < live_list[:, None], 0.0, NEG).reshape(1, slots)

    vmem = pl.BlockSpec(memory_space=pltpu.VMEM)
    hbm = pl.BlockSpec(memory_space=pl.ANY)
    smem = pl.BlockSpec(memory_space=pltpu.SMEM)
    dma = pltpu.SemaphoreType.DMA
    return pl.pallas_call(
        functools.partial(kernel, segments, cap),
        out_shape=jax.ShapeDtypeStruct((rows, cols), BF16),
        in_specs=[smem] + [vmem] * 4 + [hbm] * 2 + [vmem] * 7 + [hbm],
        out_specs=vmem,
        scratch_shapes=[
            pltpu.VMEM((2 * cols, store_rows), BF16),
            pltpu.VMEM((3, cols, width), BF16),
            pltpu.VMEM((cols, width), BF16),
            pltpu.VMEM((segments, 2 * cols, cap), BF16),
            pltpu.VMEM((segments, 2 * cols, cap), BF16),
            pltpu.VMEM((4, group, width), BF16),
            pltpu.VMEM((4, rows, group), BF16),
            pltpu.VMEM((2, 2 * rows, group), F32),
            pltpu.VMEM((rows, width), BF16),
            pltpu.VMEM((rows, width), BF16),
            pltpu.VMEM((rows, cols), BF16),
            pltpu.VMEM((3 * rows, 2 * cols), BF16),
            pltpu.VMEM((2 * cols, slots), BF16),
            pltpu.VMEM((rows, 3 * rows + slots), F32),
            pltpu.VMEM((4, rows, cols), BF16),
            pltpu.VMEM((rows + 2 * EDGE, cols), BF16),
            pltpu.VMEM((rows + 2 * EDGE, cols), F32),
            dma((3,)),
            dma((3,)),
            dma((3,)),
            dma((3,)),
            dma((3,)),
            dma((segments,)),
            dma((segments,)),
            dma((2,)),
            dma((2,)),
            dma((BLOCKS, 3)),
            dma((BLOCKS, 3)),
            dma((2,)),
            dma((2,)),
        ],
        compiler_params=pltpu.CompilerParams(
            collective_id=0, has_side_effects=True, vmem_limit_bytes=56 * 2**20
        ),
        name="segment_block",
    )(
        owner_list,
        wave_feats,
        conv_weight,
        proj_weight,
        ln_gain.reshape(1, width),
        jnp.transpose(qkv_weight, (1, 2, 0)),
        jnp.transpose(out_weight, (1, 0)),
        depth_weight,
        depth_scale.reshape(1, cols),
        depth_shift.reshape(1, cols),
        own_ids.reshape(rows, 1),
        win_ids.reshape(1, 3 * rows),
        slot_bias,
        requests,
        jnp.transpose(phrase_store, (1, 2, 0)).reshape(2 * cols, store_rows),
    )


def solution(mesh):
    in_specs = (
        P(("groups", "tm"), None),
        P(None, None, "heads"),
        P("heads", None),
        P(),
        P(None, None, "heads"),
        P(None, "heads"),
        P(None, "heads"),
        P("heads"),
        P("heads"),
        P("groups"),
        P("groups", None),
        P("groups"),
        P("tm", None, "heads"),
    )
    out_specs = P(("groups", "tm"), "heads")
    return jax.shard_map(body, mesh=mesh, in_specs=in_specs, out_specs=out_specs, check_vma=False)
```

```python
import functools
import math

import jax
import jax.numpy as jnp
from jax import lax
from jax.experimental import pallas as pl
from jax.experimental.pallas import tpu as pltpu
from jax.sharding import PartitionSpec as P

HEAD_DIM = 64
EDGE = 16
BLOCKS = 2
NEG = -1e30
F32 = jnp.float32
BF16 = jnp.bfloat16


def dot_nt(a, b):
    return lax.dot_general(a, b, (((1,), (1,)), ((), ())), preferred_element_type=F32)


def dot_nn(a, b):
    return lax.dot_general(a, b, (((1,), (0,)), ((), ())), preferred_element_type=F32)


def kernel(
    segments,
    cap,
    counts_ref,
    wave_ref,
    conv_ref,
    proj_ref,
    gain_ref,
    wqkv_hbm,
    wout_hbm,
    taps_ref,
    scale_ref,
    shift_ref,
    frame_ids_ref,
    phrase_ids_ref,
    store_hbm,
    out_ref,
    store,
    wqkv,
    wout,
    picked,
    landed,
    proj_all,
    conv_all,
    conv_pre,
    hidden,
    normed,
    queries,
    kv,
    phrases,
    bias,
    attended,
    partial,
    stats,
    mixed,
    wide,
    window,
    slot_bias,
    ranks,
    low_part,
    high_part,
    load_sem,
    proj_send,
    proj_recv,
    conv_send,
    conv_recv,
    pick_send,
    pick_recv,
    kv_send,
    kv_recv,
    att_send,
    att_recv,
    mix_send,
    mix_recv,
):
    rows, cols = out_ref.shape
    slots = phrases.shape[1]
    me = lax.axis_index("heads")
    seg = lax.axis_index("tm")
    near = me + 1 - 2 * (me % 2)
    far = (me + 2) % 4

    def remote(src, dst, send, recv, **where):
        return pltpu.make_async_remote_copy(
            src_ref=src,
            dst_ref=dst,
            send_sem=send,
            recv_sem=recv,
            device_id=where,
            device_id_type=pl.DeviceIdType.MESH,
        )

    loads = [
        pltpu.make_async_copy(store_hbm, store, load_sem.at[0]),
        pltpu.make_async_copy(wqkv_hbm, wqkv, load_sem.at[1]),
        pltpu.make_async_copy(wout_hbm, wout, load_sem.at[2]),
    ]
    for load in loads:
        load.start()

    barrier = pltpu.get_barrier_semaphore()
    for peer in (near, far):
        pl.semaphore_signal(
            barrier, inc=1, device_id={"heads": peer}, device_id_type=pl.DeviceIdType.MESH
        )
    for step in range(1, segments):
        pl.semaphore_signal(
            barrier,
            inc=1,
            device_id={"tm": (seg + step) % segments},
            device_id_type=pl.DeviceIdType.MESH,
        )
    pl.semaphore_wait(barrier, segments + 1)

    proj_copies = [
        remote(proj_ref, proj_all.at[me], proj_send.at[0], proj_recv.at[0], heads=near),
        remote(proj_ref, proj_all.at[me], proj_send.at[1], proj_recv.at[1], heads=far),
        remote(proj_all.at[far], proj_all.at[far], proj_send.at[2], proj_recv.at[2], heads=near),
    ]
    proj_copies[1].start()
    proj_copies[0].start()
    proj_all[me] = proj_ref[...]

    store_rows = store.shape[1]
    ids = phrase_ids_ref[...]
    offset = ids - seg * store_rows
    held = jnp.logical_and(offset >= 0, offset < store_rows)
    list_shape = (slots, slots)
    earlier = lax.broadcasted_iota(jnp.int32, list_shape, 0) < lax.broadcasted_iota(
        jnp.int32, list_shape, 1
    )
    rank = dot_nn(jnp.where(held, 1.0, 0.0).astype(BF16), jnp.where(earlier, 1.0, 0.0).astype(BF16))
    ranks[...] = jnp.where(held, rank, -1.0)
    offset = jnp.where(held, offset, 0)
    low_part[...] = (offset & 255).astype(F32)
    high_part[...] = lax.shift_right_logical(offset, 8).astype(F32)

    def pick_step(turn):
        return lax.rem(segments // 2 + turn, segments)

    def pick(turn, carry):
        target = lax.rem(seg + pick_step(turn), segments)
        line = pl.ds(target, 1)
        slot = lax.broadcasted_iota(jnp.int32, (cap, slots), 0).astype(F32)
        match = jnp.where(slot == ranks[line, :], 1.0, 0.0).astype(BF16)
        lower = jnp.broadcast_to(low_part[line, :], (8, slots)).astype(BF16)
        upper = jnp.broadcast_to(high_part[line, :], (8, slots)).astype(BF16)
        wanted = dot_nt(lower, match) + 256.0 * dot_nt(upper, match)
        place = lax.broadcasted_iota(jnp.int32, (store_rows, cap), 0)
        hot = jnp.where(place == wanted[0:1, :].astype(jnp.int32), 1.0, 0.0).astype(BF16)
        picked[target] = dot_nn(store[...], hot).astype(BF16)
        return carry

    def pick_copy(turn):
        step = pick_step(turn)
        target = lax.rem(seg + step, segments)
        return remote(
            picked.at[target], landed.at[seg], pick_send.at[step], pick_recv.at[step], tm=target
        )

    own_turn = segments - segments // 2
    early = max(1, segments // 4)
    loads[0].wait()
    lax.fori_loop(0, early, pick, 0)

    def send_pick(turn, carry):
        pick_copy(turn).start()
        return carry

    lax.fori_loop(0, early, send_pick, 0)

    group = conv_ref.shape[2]
    both = jnp.concatenate([conv_ref[0], conv_ref[1]], axis=1)
    taps_out = dot_nn(wave_ref[...], both)
    conv_pre[0] = taps_out[:, :group]
    conv_pre[1] = taps_out[:, group:]
    total = conv_pre[0, pl.ds(0, rows, stride=2), :] + conv_pre[1, pl.ds(1, rows, stride=2), :]
    gelu = 0.5 * total * (1.0 + lax.erf(total * math.sqrt(0.5)))
    conv_all[me] = gelu.astype(BF16)
    conv_copies = [
        remote(conv_all.at[me], conv_all.at[me], conv_send.at[0], conv_recv.at[0], heads=near),
        remote(conv_all.at[me], conv_all.at[me], conv_send.at[1], conv_recv.at[1], heads=far),
        remote(conv_all.at[far], conv_all.at[far], conv_send.at[2], conv_recv.at[2], heads=near),
    ]
    conv_copies[1].start()
    conv_copies[0].start()

    lax.fori_loop(early, segments, pick, 0)
    landed[seg] = picked[seg]

    own_line = frame_ids_ref[pl.ds(seg, 1), :]
    prev_line = frame_ids_ref[pl.ds(jnp.maximum(seg - 1, 0), 1), :]
    next_line = frame_ids_ref[pl.ds(jnp.minimum(seg + 1, segments - 1), 1), :]
    window[:, :rows] = jnp.where(seg > 0, prev_line, -1)
    window[:, rows : 2 * rows] = own_line
    window[:, 2 * rows :] = jnp.where(seg < segments - 1, next_line, -1)
    square = (rows, rows)
    diagonal = lax.broadcasted_iota(jnp.int32, square, 0) == lax.broadcasted_iota(
        jnp.int32, square, 1
    )
    own_column = jnp.sum(
        jnp.where(diagonal, own_line.astype(F32), 0.0), axis=1, keepdims=True
    ).astype(jnp.int32)
    bias[...] = jnp.where(own_column == window[...], 0.0, NEG)

    my_ids = phrase_ids_ref[pl.ds(seg, 1), :]
    live = lax.broadcasted_iota(jnp.int32, (1, slots), 1) < counts_ref[seg]
    owners = []
    least = 0
    for use in range(slots // cap):
        smallest = jnp.min(jnp.where(my_ids >= least, my_ids, segments * store_rows - 1))
        owner = smallest // store_rows
        owners.append(owner)
        least = (owner + 1) * store_rows
        listed = jnp.logical_and(my_ids >= owner * store_rows, my_ids < least)
        number = jnp.sum(
            jnp.where(jnp.logical_and(listed, live), 1.0, 0.0), axis=1, keepdims=True
        )
        place = lax.broadcasted_iota(jnp.int32, (1, cap), 1).astype(F32)
        slot_bias[:, use * cap : (use + 1) * cap] = jnp.where(place < number, 0.0, NEG)

    conv_copies[1].wait_recv()
    conv_copies[2].start()
    proj_copies[1].wait_recv()
    proj_copies[2].start()
    conv_copies[0].wait_recv()
    proj_copies[0].wait_recv()
    conv_copies[2].wait_recv()
    proj_copies[2].wait_recv()
    conv_full = jnp.concatenate([conv_all[r] for r in range(4)], axis=1)
    weight_full = proj_all[...].reshape(4 * group, proj_ref.shape[1])
    hidden[...] = dot_nn(conv_full, weight_full).astype(BF16)

    def norm(block, carry):
        at = pl.ds(pl.multiple_of(block * 64, 64), 64)
        values = hidden[at, :].astype(F32)
        centred = values - jnp.mean(values, axis=-1, keepdims=True)
        variance = jnp.mean(centred * centred, axis=-1, keepdims=True)
        normed[at, :] = (centred * lax.rsqrt(variance + 1e-05) * gain_ref[...][None, :]).astype(BF16)
        return carry

    lax.fori_loop(0, rows // 64, norm, 0)

    loads[1].wait()
    kv[rows : 2 * rows, :cols] = dot_nt(normed[...], wqkv[1]).astype(BF16)
    kv[rows : 2 * rows, cols:] = dot_nt(normed[...], wqkv[2]).astype(BF16)
    own_kv = kv.at[pl.ds(rows, rows)]
    kv_down = remote(
        own_kv, kv.at[pl.ds(0, rows)], kv_send.at[0], kv_recv.at[0], tm=(seg + 1) % segments
    )
    kv_up = remote(
        own_kv,
        kv.at[pl.ds(2 * rows, rows)],
        kv_send.at[1],
        kv_recv.at[1],
        tm=(seg + segments - 1) % segments,
    )
    first = seg == 0
    last = seg == segments - 1
    inner_low = seg > 0
    inner_high = seg < segments - 1

    @pl.when(inner_high)
    def _():
        kv_down.start()

    @pl.when(inner_low)
    def _():
        kv_up.start()

    @pl.when(first)
    def _():
        kv[:rows, :] = jnp.zeros((rows, 2 * cols), BF16)

    @pl.when(last)
    def _():
        kv[2 * rows :, :] = jnp.zeros((rows, 2 * cols), BF16)

    def send_late(turn, carry):
        @pl.when(turn != own_turn)
        def _():
            pick_copy(turn).start()

        return carry

    lax.fori_loop(early, segments, send_late, 0)

    queries[...] = (dot_nt(normed[...], wqkv[0]).astype(BF16) * HEAD_DIM**-0.5).astype(BF16)

    @pl.when(inner_low)
    def _():
        kv_down.wait_recv()

    @pl.when(inner_high)
    def _():
        kv_up.wait_recv()

    heads = cols // HEAD_DIM
    step_rows = rows // BLOCKS

    def attend_frames(block, carry):
        at = pl.ds(pl.multiple_of(block * step_rows, 32), step_rows)
        for head in range(heads):
            low, high = head * HEAD_DIM, (head + 1) * HEAD_DIM
            scores = dot_nt(queries[at, low:high], kv[:, low:high]) + bias[at, :]
            highest = jnp.max(scores, axis=-1, keepdims=True)
            raised = jnp.exp(scores - highest)
            stats[head, 0, at, :] = highest
            stats[head, 1, at, :] = jnp.sum(raised, axis=-1, keepdims=True)
            partial[head, at, :] = dot_nn(raised.astype(BF16), kv[:, cols + low : cols + high])
        return carry

    lax.fori_loop(0, BLOCKS, attend_frames, 0)

    def wait_pick(step, carry):
        pick_copy(lax.rem(step + own_turn, segments)).wait_recv()
        return carry

    lax.fori_loop(1, segments, wait_pick, 0)
    for use, owner in enumerate(owners):
        phrases[:, use * cap : (use + 1) * cap] = landed[owner]

    def att_copies(block):
        at = pl.ds(pl.multiple_of(block * step_rows, 32), step_rows)
        mine, others = attended.at[me, at], attended.at[far, at]
        return [
            remote(mine, mine, att_send.at[block, 0], att_recv.at[block, 0], heads=near),
            remote(mine, mine, att_send.at[block, 1], att_recv.at[block, 1], heads=far),
            remote(others, others, att_send.at[block, 2], att_recv.at[block, 2], heads=near),
        ]

    def forward(block):
        copies = att_copies(block)
        copies[1].wait_recv()
        copies[2].start()

    def attend(block, carry):
        at = pl.ds(pl.multiple_of(block * step_rows, 32), step_rows)
        for head in range(heads):
            low, high = head * HEAD_DIM, (head + 1) * HEAD_DIM
            scores = dot_nn(queries[at, low:high], phrases[low:high, :]) + slot_bias[...]
            before = stats[head, 0, at, :]
            highest = jnp.maximum(before, jnp.max(scores, axis=-1, keepdims=True))
            raised = jnp.exp(scores - highest)
            shrink = jnp.exp(before - highest)
            whole = stats[head, 1, at, :] * shrink + jnp.sum(raised, axis=-1, keepdims=True)
            summed = partial[head, at, :] * shrink + dot_nt(
                raised.astype(BF16), phrases[cols + low : cols + high, :]
            )
            attended[me, at, low:high] = (summed / whole).astype(BF16)
        copies = att_copies(block)
        copies[1].start()
        copies[0].start()

        @pl.when(block > 0)
        def _():
            forward(block - 1)

        return carry

    lax.fori_loop(0, BLOCKS, attend, 0)
    forward(BLOCKS - 1)

    loads[2].wait()
    own = hidden[:, :cols]
    for r in range(1, 4):
        own = jnp.where(me == r, hidden[:, r * cols : (r + 1) * cols], own)
    for block in range(BLOCKS):
        copies = att_copies(block)
        copies[0].wait_recv()
        copies[2].wait_recv()
    attended_full = jnp.concatenate([attended[r] for r in range(4)], axis=1)
    product = dot_nt(attended_full, wout[...])
    mixed[EDGE : EDGE + rows, :] = (own.astype(F32) + product).astype(BF16)

    mix_down = remote(
        mixed.at[pl.ds(rows, EDGE)],
        mixed.at[pl.ds(0, EDGE)],
        mix_send.at[0],
        mix_recv.at[0],
        tm=(seg + 1) % segments,
    )
    mix_up = remote(
        mixed.at[pl.ds(EDGE, EDGE)],
        mixed.at[pl.ds(EDGE + rows, EDGE)],
        mix_send.at[1],
        mix_recv.at[1],
        tm=(seg + segments - 1) % segments,
    )

    @pl.when(inner_high)
    def _():
        mix_down.start()

    @pl.when(inner_low)
    def _():
        mix_up.start()

    @pl.when(first)
    def _():
        mixed[:EDGE, :] = jnp.zeros((EDGE, cols), BF16)

    @pl.when(last)
    def _():
        mixed[EDGE + rows :, :] = jnp.zeros((EDGE, cols), BF16)

    wide[EDGE : EDGE + rows, :] = mixed[EDGE : EDGE + rows, :].astype(F32)

    for copy in proj_copies + conv_copies:
        copy.wait_send()

    def wait_sent(step, carry):
        pick_copy(lax.rem(step + own_turn, segments)).wait_send()
        return carry

    lax.fori_loop(1, segments, wait_sent, 0)
    for block in range(BLOCKS):
        for copy in att_copies(block):
            copy.wait_send()

    @pl.when(inner_high)
    def _():
        kv_down.wait_send()
        mix_down.wait_send()
        mix_up.wait_recv()

    @pl.when(inner_low)
    def _():
        kv_up.wait_send()
        mix_up.wait_send()
        mix_down.wait_recv()

    wide[:EDGE, :] = mixed[:EDGE, :].astype(F32)
    wide[EDGE + rows :, :] = mixed[EDGE + rows :, :].astype(F32)

    kernel_taps = taps_ref.shape[0]
    lead = EDGE - kernel_taps // 2
    for top in range(0, rows, 64):
        depth = jnp.zeros((64, cols), F32)
        for tap in range(kernel_taps):
            start = top + tap + lead
            depth = depth + wide[start : start + 64, :] * taps_ref[tap : tap + 1, :]
        gated = depth * scale_ref[...][None, :] + shift_ref[...][None, :]
        value = wide[EDGE + top : EDGE + top + 64, :] + gated / (1.0 + jnp.exp(-gated))
        out_ref[top : top + 64, :] = value.astype(BF16)


def body(
    wave_feats,
    conv_weight,
    proj_weight,
    ln_gain,
    qkv_weight,
    out_weight,
    depth_weight,
    depth_scale,
    depth_shift,
    seg_ids,
    phrase_ids,
    counts,
    phrase_store,
):
    rows = wave_feats.shape[0] // 2
    cols = qkv_weight.shape[2]
    width = qkv_weight.shape[0]
    group = proj_weight.shape[0]
    segments = lax.axis_size("tm")
    slots = phrase_ids.shape[1]
    cap = 2 * slots // segments
    store_rows = phrase_store.shape[0]

    vmem = pl.BlockSpec(memory_space=pltpu.VMEM)
    hbm = pl.BlockSpec(memory_space=pl.ANY)
    smem = pl.BlockSpec(memory_space=pltpu.SMEM)
    dma = pltpu.SemaphoreType.DMA
    return pl.pallas_call(
        functools.partial(kernel, segments, cap),
        out_shape=jax.ShapeDtypeStruct((rows, cols), BF16),
        in_specs=[smem] + [vmem] * 4 + [hbm] * 2 + [vmem] * 5 + [hbm],
        out_specs=vmem,
        scratch_shapes=[
            pltpu.VMEM((2 * cols, store_rows), BF16),
            pltpu.VMEM((3, cols, width), BF16),
            pltpu.VMEM((cols, width), BF16),
            pltpu.VMEM((segments, 2 * cols, cap), BF16),
            pltpu.VMEM((segments, 2 * cols, cap), BF16),
            pltpu.VMEM((4, group, width), BF16),
            pltpu.VMEM((4, rows, group), BF16),
            pltpu.VMEM((2, 2 * rows, group), F32),
            pltpu.VMEM((rows, width), BF16),
            pltpu.VMEM((rows, width), BF16),
            pltpu.VMEM((rows, cols), BF16),
            pltpu.VMEM((3 * rows, 2 * cols), BF16),
            pltpu.VMEM((2 * cols, slots), BF16),
            pltpu.VMEM((rows, 3 * rows), F32),
            pltpu.VMEM((4, rows, cols), BF16),
            pltpu.VMEM((cols // HEAD_DIM, rows, HEAD_DIM), F32),
            pltpu.VMEM((cols // HEAD_DIM, 2, rows, 1), F32),
            pltpu.VMEM((rows + 2 * EDGE, cols), BF16),
            pltpu.VMEM((rows + 2 * EDGE, cols), F32),
            pltpu.VMEM((1, 3 * rows), jnp.int32),
            pltpu.VMEM((1, slots), F32),
            pltpu.VMEM((segments, slots), F32),
            pltpu.VMEM((segments, slots), F32),
            pltpu.VMEM((segments, slots), F32),
            dma((3,)),
            dma((3,)),
            dma((3,)),
            dma((3,)),
            dma((3,)),
            dma((segments,)),
            dma((segments,)),
            dma((2,)),
            dma((2,)),
            dma((BLOCKS, 3)),
            dma((BLOCKS, 3)),
            dma((2,)),
            dma((2,)),
        ],
        compiler_params=pltpu.CompilerParams(
            collective_id=0, has_side_effects=True, vmem_limit_bytes=56 * 2**20
        ),
        name="segment_block",
    )(
        counts,
        wave_feats,
        conv_weight,
        proj_weight,
        ln_gain,
        jnp.transpose(qkv_weight, (1, 2, 0)),
        jnp.transpose(out_weight, (1, 0)),
        depth_weight,
        depth_scale,
        depth_shift,
        seg_ids.reshape(segments, rows),
        phrase_ids,
        jnp.transpose(phrase_store, (1, 2, 0)).reshape(2 * cols, store_rows),
    )


def solution(mesh):
    in_specs = (
        P(("groups", "tm"), None),
        P(None, None, "heads"),
        P("heads", None),
        P(),
        P(None, None, "heads"),
        P(None, "heads"),
        P(None, "heads"),
        P("heads"),
        P("heads"),
        P("groups"),
        P("groups", None),
        P("groups"),
        P("tm", None, "heads"),
    )
    out_specs = P(("groups", "tm"), "heads")
    return jax.shard_map(body, mesh=mesh, in_specs=in_specs, out_specs=out_specs, check_vma=False)
```

```python
import functools
import math

import jax
import jax.numpy as jnp
from jax import lax
from jax.experimental import pallas as pl
from jax.experimental.pallas import tpu as pltpu
from jax.sharding import PartitionSpec as P

HEAD_DIM = 64
EDGE = 16
BLOCKS = 2
NEG = -1e30
F32 = jnp.float32
BF16 = jnp.bfloat16


def dot_nt(a, b):
    return lax.dot_general(a, b, (((1,), (1,)), ((), ())), preferred_element_type=F32)


def dot_nn(a, b):
    return lax.dot_general(a, b, (((1,), (0,)), ((), ())), preferred_element_type=F32)


def kernel(
    segments,
    cap,
    counts_ref,
    wave_ref,
    conv_ref,
    proj_ref,
    gain_ref,
    wqkv_hbm,
    wout_hbm,
    taps_ref,
    scale_ref,
    shift_ref,
    frame_ids_ref,
    phrase_ids_ref,
    store_hbm,
    out_ref,
    store,
    wqkv,
    wout,
    picked,
    landed,
    proj_all,
    conv_all,
    conv_pre,
    hidden,
    normed,
    queries,
    kv,
    phrases,
    bias,
    attended,
    partial,
    stats,
    mixed,
    wide,
    window,
    slot_bias,
    ranks,
    low_part,
    high_part,
    load_sem,
    proj_send,
    proj_recv,
    conv_send,
    conv_recv,
    pick_send,
    pick_recv,
    kv_send,
    kv_recv,
    att_send,
    att_recv,
    mix_send,
    mix_recv,
):
    rows, cols = out_ref.shape
    slots = phrases.shape[1]
    me = lax.axis_index("heads")
    seg = lax.axis_index("tm")
    near = me + 1 - 2 * (me % 2)
    far = (me + 2) % 4

    def remote(src, dst, send, recv, **where):
        return pltpu.make_async_remote_copy(
            src_ref=src,
            dst_ref=dst,
            send_sem=send,
            recv_sem=recv,
            device_id=where,
            device_id_type=pl.DeviceIdType.MESH,
        )

    loads = [
        pltpu.make_async_copy(store_hbm, store, load_sem.at[0]),
        pltpu.make_async_copy(wqkv_hbm, wqkv, load_sem.at[1]),
        pltpu.make_async_copy(wout_hbm, wout, load_sem.at[2]),
    ]
    for load in loads:
        load.start()

    barrier = pltpu.get_barrier_semaphore()
    for peer in (near, far):
        pl.semaphore_signal(
            barrier, inc=1, device_id={"heads": peer}, device_id_type=pl.DeviceIdType.MESH
        )
    for step in range(1, segments):
        pl.semaphore_signal(
            barrier,
            inc=1,
            device_id={"tm": (seg + step) % segments},
            device_id_type=pl.DeviceIdType.MESH,
        )
    pl.semaphore_wait(barrier, segments + 1)

    proj_copies = [
        remote(proj_ref, proj_all.at[me], proj_send.at[0], proj_recv.at[0], heads=near),
        remote(proj_ref, proj_all.at[me], proj_send.at[1], proj_recv.at[1], heads=far),
        remote(proj_all.at[far], proj_all.at[far], proj_send.at[2], proj_recv.at[2], heads=near),
    ]
    proj_copies[1].start()
    proj_copies[0].start()
    proj_all[me] = proj_ref[...]

    store_rows = store.shape[1]
    ids = phrase_ids_ref[...]
    offset = ids - seg * store_rows
    held = jnp.logical_and(offset >= 0, offset < store_rows)
    list_shape = (slots, slots)
    earlier = lax.broadcasted_iota(jnp.int32, list_shape, 0) < lax.broadcasted_iota(
        jnp.int32, list_shape, 1
    )
    rank = dot_nn(jnp.where(held, 1.0, 0.0).astype(BF16), jnp.where(earlier, 1.0, 0.0).astype(BF16))
    ranks[...] = jnp.where(held, rank, -1.0)
    offset = jnp.where(held, offset, 0)
    low_part[...] = (offset & 255).astype(F32)
    high_part[...] = lax.shift_right_logical(offset, 8).astype(F32)

    def pick_step(turn):
        return lax.rem(segments // 2 + turn, segments)

    def pick(turn, carry):
        target = lax.rem(seg + pick_step(turn), segments)
        line = pl.ds(target, 1)
        slot = lax.broadcasted_iota(jnp.int32, (cap, slots), 0).astype(F32)
        match = jnp.where(slot == ranks[line, :], 1.0, 0.0).astype(BF16)
        lower = jnp.broadcast_to(low_part[line, :], (8, slots)).astype(BF16)
        upper = jnp.broadcast_to(high_part[line, :], (8, slots)).astype(BF16)
        wanted = dot_nt(lower, match) + 256.0 * dot_nt(upper, match)
        place = lax.broadcasted_iota(jnp.int32, (store_rows, cap), 0)
        hot = jnp.where(place == wanted[0:1, :].astype(jnp.int32), 1.0, 0.0).astype(BF16)
        picked[target] = dot_nn(store[...], hot).astype(BF16)
        return carry

    def pick_copy(turn):
        step = pick_step(turn)
        target = lax.rem(seg + step, segments)
        return remote(
            picked.at[target], landed.at[seg], pick_send.at[step], pick_recv.at[step], tm=target
        )

    own_turn = segments - segments // 2
    early = max(1, segments // 4)
    loads[0].wait()
    lax.fori_loop(0, early, pick, 0)

    def send_pick(turn, carry):
        pick_copy(turn).start()
        return carry

    lax.fori_loop(0, early, send_pick, 0)

    group = conv_ref.shape[2]
    both = jnp.concatenate([conv_ref[0], conv_ref[1]], axis=1)
    taps_out = dot_nn(wave_ref[...], both)
    conv_pre[0] = taps_out[:, :group]
    conv_pre[1] = taps_out[:, group:]
    total = conv_pre[0, pl.ds(0, rows, stride=2), :] + conv_pre[1, pl.ds(1, rows, stride=2), :]
    gelu = 0.5 * total * (1.0 + lax.erf(total * math.sqrt(0.5)))
    conv_all[me] = gelu.astype(BF16)
    conv_copies = [
        remote(conv_all.at[me], conv_all.at[me], conv_send.at[0], conv_recv.at[0], heads=near),
        remote(conv_all.at[me], conv_all.at[me], conv_send.at[1], conv_recv.at[1], heads=far),
        remote(conv_all.at[far], conv_all.at[far], conv_send.at[2], conv_recv.at[2], heads=near),
    ]
    conv_copies[1].start()
    conv_copies[0].start()

    def pick_send_on(turn, carry):
        pick(turn, carry)

        @pl.when(turn != own_turn)
        def _():
            pick_copy(turn).start()

        return carry

    lax.fori_loop(early, segments // 2, pick_send_on, 0)
    lax.fori_loop(segments // 2, segments, pick, 0)
    landed[seg] = picked[seg]

    own_line = frame_ids_ref[pl.ds(seg, 1), :]
    prev_line = frame_ids_ref[pl.ds(jnp.maximum(seg - 1, 0), 1), :]
    next_line = frame_ids_ref[pl.ds(jnp.minimum(seg + 1, segments - 1), 1), :]
    window[:, :rows] = jnp.where(seg > 0, prev_line, -1)
    window[:, rows : 2 * rows] = own_line
    window[:, 2 * rows :] = jnp.where(seg < segments - 1, next_line, -1)
    square = (rows, rows)
    diagonal = lax.broadcasted_iota(jnp.int32, square, 0) == lax.broadcasted_iota(
        jnp.int32, square, 1
    )
    own_column = jnp.sum(
        jnp.where(diagonal, own_line.astype(F32), 0.0), axis=1, keepdims=True
    ).astype(jnp.int32)
    bias[...] = jnp.where(own_column == window[...], 0.0, NEG)

    my_ids = phrase_ids_ref[pl.ds(seg, 1), :]
    live = lax.broadcasted_iota(jnp.int32, (1, slots), 1) < counts_ref[seg]
    owners = []
    least = 0
    for use in range(slots // cap):
        smallest = jnp.min(jnp.where(my_ids >= least, my_ids, segments * store_rows - 1))
        owner = smallest // store_rows
        owners.append(owner)
        least = (owner + 1) * store_rows
        listed = jnp.logical_and(my_ids >= owner * store_rows, my_ids < least)
        number = jnp.sum(
            jnp.where(jnp.logical_and(listed, live), 1.0, 0.0), axis=1, keepdims=True
        )
        place = lax.broadcasted_iota(jnp.int32, (1, cap), 1).astype(F32)
        slot_bias[:, use * cap : (use + 1) * cap] = jnp.where(place < number, 0.0, NEG)

    conv_copies[1].wait_recv()
    conv_copies[2].start()
    proj_copies[1].wait_recv()
    proj_copies[2].start()
    conv_copies[0].wait_recv()
    proj_copies[0].wait_recv()
    conv_copies[2].wait_recv()
    proj_copies[2].wait_recv()
    conv_full = jnp.concatenate([conv_all[r] for r in range(4)], axis=1)
    weight_full = proj_all[...].reshape(4 * group, proj_ref.shape[1])
    hidden[...] = dot_nn(conv_full, weight_full).astype(BF16)

    def norm(block, carry):
        at = pl.ds(pl.multiple_of(block * 64, 64), 64)
        values = hidden[at, :].astype(F32)
        centred = values - jnp.mean(values, axis=-1, keepdims=True)
        variance = jnp.mean(centred * centred, axis=-1, keepdims=True)
        normed[at, :] = (centred * lax.rsqrt(variance + 1e-05) * gain_ref[...][None, :]).astype(BF16)
        return carry

    lax.fori_loop(0, rows // 64, norm, 0)

    loads[1].wait()
    kv[rows : 2 * rows, :cols] = dot_nt(normed[...], wqkv[1]).astype(BF16)
    kv[rows : 2 * rows, cols:] = dot_nt(normed[...], wqkv[2]).astype(BF16)
    own_kv = kv.at[pl.ds(rows, rows)]
    kv_down = remote(
        own_kv, kv.at[pl.ds(0, rows)], kv_send.at[0], kv_recv.at[0], tm=(seg + 1) % segments
    )
    kv_up = remote(
        own_kv,
        kv.at[pl.ds(2 * rows, rows)],
        kv_send.at[1],
        kv_recv.at[1],
        tm=(seg + segments - 1) % segments,
    )
    first = seg == 0
    last = seg == segments - 1
    inner_low = seg > 0
    inner_high = seg < segments - 1

    @pl.when(inner_high)
    def _():
        kv_down.start()

    @pl.when(inner_low)
    def _():
        kv_up.start()

    @pl.when(first)
    def _():
        kv[:rows, :] = jnp.zeros((rows, 2 * cols), BF16)

    @pl.when(last)
    def _():
        kv[2 * rows :, :] = jnp.zeros((rows, 2 * cols), BF16)

    def send_late(turn, carry):
        @pl.when(turn != own_turn)
        def _():
            pick_copy(turn).start()

        return carry

    lax.fori_loop(segments // 2, segments, send_late, 0)

    queries[...] = (dot_nt(normed[...], wqkv[0]).astype(BF16) * HEAD_DIM**-0.5).astype(BF16)

    @pl.when(inner_low)
    def _():
        kv_down.wait_recv()

    @pl.when(inner_high)
    def _():
        kv_up.wait_recv()

    heads = cols // HEAD_DIM
    step_rows = rows // BLOCKS

    def attend_frames(block, carry):
        at = pl.ds(pl.multiple_of(block * step_rows, 32), step_rows)
        for head in range(heads):
            low, high = head * HEAD_DIM, (head + 1) * HEAD_DIM
            scores = dot_nt(queries[at, low:high], kv[:, low:high]) + bias[at, :]
            highest = jnp.max(scores, axis=-1, keepdims=True)
            raised = jnp.exp(scores - highest)
            stats[head, 0, at, :] = highest
            stats[head, 1, at, :] = jnp.sum(raised, axis=-1, keepdims=True)
            partial[head, at, :] = dot_nn(raised.astype(BF16), kv[:, cols + low : cols + high])
        return carry

    lax.fori_loop(0, BLOCKS, attend_frames, 0)

    def wait_pick(step, carry):
        pick_copy(lax.rem(step + own_turn, segments)).wait_recv()
        return carry

    lax.fori_loop(1, segments, wait_pick, 0)
    for use, owner in enumerate(owners):
        phrases[:, use * cap : (use + 1) * cap] = landed[owner]

    def att_copies(block):
        at = pl.ds(pl.multiple_of(block * step_rows, 32), step_rows)
        mine, others = attended.at[me, at], attended.at[far, at]
        return [
            remote(mine, mine, att_send.at[block, 0], att_recv.at[block, 0], heads=near),
            remote(mine, mine, att_send.at[block, 1], att_recv.at[block, 1], heads=far),
            remote(others, others, att_send.at[block, 2], att_recv.at[block, 2], heads=near),
        ]

    def forward(block):
        copies = att_copies(block)
        copies[1].wait_recv()
        copies[2].start()

    def attend(block, carry):
        at = pl.ds(pl.multiple_of(block * step_rows, 32), step_rows)
        for head in range(heads):
            low, high = head * HEAD_DIM, (head + 1) * HEAD_DIM
            scores = dot_nn(queries[at, low:high], phrases[low:high, :]) + slot_bias[...]
            before = stats[head, 0, at, :]
            highest = jnp.maximum(before, jnp.max(scores, axis=-1, keepdims=True))
            raised = jnp.exp(scores - highest)
            shrink = jnp.exp(before - highest)
            whole = stats[head, 1, at, :] * shrink + jnp.sum(raised, axis=-1, keepdims=True)
            summed = partial[head, at, :] * shrink + dot_nt(
                raised.astype(BF16), phrases[cols + low : cols + high, :]
            )
            attended[me, at, low:high] = (summed / whole).astype(BF16)
        copies = att_copies(block)
        copies[1].start()
        copies[0].start()

        @pl.when(block > 0)
        def _():
            forward(block - 1)

        return carry

    lax.fori_loop(0, BLOCKS, attend, 0)
    forward(BLOCKS - 1)

    loads[2].wait()
    own = hidden[:, :cols]
    for r in range(1, 4):
        own = jnp.where(me == r, hidden[:, r * cols : (r + 1) * cols], own)
    for block in range(BLOCKS):
        copies = att_copies(block)
        copies[0].wait_recv()
        copies[2].wait_recv()
    attended_full = jnp.concatenate([attended[r] for r in range(4)], axis=1)
    product = dot_nt(attended_full, wout[...])
    mixed[EDGE : EDGE + rows, :] = (own.astype(F32) + product).astype(BF16)

    mix_down = remote(
        mixed.at[pl.ds(rows, EDGE)],
        mixed.at[pl.ds(0, EDGE)],
        mix_send.at[0],
        mix_recv.at[0],
        tm=(seg + 1) % segments,
    )
    mix_up = remote(
        mixed.at[pl.ds(EDGE, EDGE)],
        mixed.at[pl.ds(EDGE + rows, EDGE)],
        mix_send.at[1],
        mix_recv.at[1],
        tm=(seg + segments - 1) % segments,
    )

    @pl.when(inner_high)
    def _():
        mix_down.start()

    @pl.when(inner_low)
    def _():
        mix_up.start()

    @pl.when(first)
    def _():
        mixed[:EDGE, :] = jnp.zeros((EDGE, cols), BF16)

    @pl.when(last)
    def _():
        mixed[EDGE + rows :, :] = jnp.zeros((EDGE, cols), BF16)

    wide[EDGE : EDGE + rows, :] = mixed[EDGE : EDGE + rows, :].astype(F32)

    for copy in proj_copies + conv_copies:
        copy.wait_send()

    def wait_sent(step, carry):
        pick_copy(lax.rem(step + own_turn, segments)).wait_send()
        return carry

    lax.fori_loop(1, segments, wait_sent, 0)
    for block in range(BLOCKS):
        for copy in att_copies(block):
            copy.wait_send()

    @pl.when(inner_high)
    def _():
        kv_down.wait_send()
        mix_down.wait_send()
        mix_up.wait_recv()

    @pl.when(inner_low)
    def _():
        kv_up.wait_send()
        mix_up.wait_send()
        mix_down.wait_recv()

    wide[:EDGE, :] = mixed[:EDGE, :].astype(F32)
    wide[EDGE + rows :, :] = mixed[EDGE + rows :, :].astype(F32)

    kernel_taps = taps_ref.shape[0]
    lead = EDGE - kernel_taps // 2
    for top in range(0, rows, 64):
        depth = jnp.zeros((64, cols), F32)
        for tap in range(kernel_taps):
            start = top + tap + lead
            depth = depth + wide[start : start + 64, :] * taps_ref[tap : tap + 1, :]
        gated = depth * scale_ref[...][None, :] + shift_ref[...][None, :]
        value = wide[EDGE + top : EDGE + top + 64, :] + gated / (1.0 + jnp.exp(-gated))
        out_ref[top : top + 64, :] = value.astype(BF16)


def body(
    wave_feats,
    conv_weight,
    proj_weight,
    ln_gain,
    qkv_weight,
    out_weight,
    depth_weight,
    depth_scale,
    depth_shift,
    seg_ids,
    phrase_ids,
    counts,
    phrase_store,
):
    rows = wave_feats.shape[0] // 2
    cols = qkv_weight.shape[2]
    width = qkv_weight.shape[0]
    group = proj_weight.shape[0]
    segments = lax.axis_size("tm")
    slots = phrase_ids.shape[1]
    cap = 2 * slots // segments
    store_rows = phrase_store.shape[0]

    vmem = pl.BlockSpec(memory_space=pltpu.VMEM)
    hbm = pl.BlockSpec(memory_space=pl.ANY)
    smem = pl.BlockSpec(memory_space=pltpu.SMEM)
    dma = pltpu.SemaphoreType.DMA
    return pl.pallas_call(
        functools.partial(kernel, segments, cap),
        out_shape=jax.ShapeDtypeStruct((rows, cols), BF16),
        in_specs=[smem] + [vmem] * 4 + [hbm] * 2 + [vmem] * 5 + [hbm],
        out_specs=vmem,
        scratch_shapes=[
            pltpu.VMEM((2 * cols, store_rows), BF16),
            pltpu.VMEM((3, cols, width), BF16),
            pltpu.VMEM((cols, width), BF16),
            pltpu.VMEM((segments, 2 * cols, cap), BF16),
            pltpu.VMEM((segments, 2 * cols, cap), BF16),
            pltpu.VMEM((4, group, width), BF16),
            pltpu.VMEM((4, rows, group), BF16),
            pltpu.VMEM((2, 2 * rows, group), F32),
            pltpu.VMEM((rows, width), BF16),
            pltpu.VMEM((rows, width), BF16),
            pltpu.VMEM((rows, cols), BF16),
            pltpu.VMEM((3 * rows, 2 * cols), BF16),
            pltpu.VMEM((2 * cols, slots), BF16),
            pltpu.VMEM((rows, 3 * rows), F32),
            pltpu.VMEM((4, rows, cols), BF16),
            pltpu.VMEM((cols // HEAD_DIM, rows, HEAD_DIM), F32),
            pltpu.VMEM((cols // HEAD_DIM, 2, rows, 1), F32),
            pltpu.VMEM((rows + 2 * EDGE, cols), BF16),
            pltpu.VMEM((rows + 2 * EDGE, cols), F32),
            pltpu.VMEM((1, 3 * rows), jnp.int32),
            pltpu.VMEM((1, slots), F32),
            pltpu.VMEM((segments, slots), F32),
            pltpu.VMEM((segments, slots), F32),
            pltpu.VMEM((segments, slots), F32),
            dma((3,)),
            dma((3,)),
            dma((3,)),
            dma((3,)),
            dma((3,)),
            dma((segments,)),
            dma((segments,)),
            dma((2,)),
            dma((2,)),
            dma((BLOCKS, 3)),
            dma((BLOCKS, 3)),
            dma((2,)),
            dma((2,)),
        ],
        compiler_params=pltpu.CompilerParams(
            collective_id=0, has_side_effects=True, vmem_limit_bytes=56 * 2**20
        ),
        name="segment_block",
    )(
        counts,
        wave_feats,
        conv_weight,
        proj_weight,
        ln_gain,
        jnp.transpose(qkv_weight, (1, 2, 0)),
        jnp.transpose(out_weight, (1, 0)),
        depth_weight,
        depth_scale,
        depth_shift,
        seg_ids.reshape(segments, rows),
        phrase_ids,
        jnp.transpose(phrase_store, (1, 2, 0)).reshape(2 * cols, store_rows),
    )


def solution(mesh):
    in_specs = (
        P(("groups", "tm"), None),
        P(None, None, "heads"),
        P("heads", None),
        P(),
        P(None, None, "heads"),
        P(None, "heads"),
        P(None, "heads"),
        P("heads"),
        P("heads"),
        P("groups"),
        P("groups", None),
        P("groups"),
        P("tm", None, "heads"),
    )
    out_specs = P(("groups", "tm"), "heads")
    return jax.shard_map(body, mesh=mesh, in_specs=in_specs, out_specs=out_specs, check_vma=False)
```
